512 devices in a mesh: row: 16 (over y, core), col: 16 (over z, x_hi), bin: 2 (over x_lo).
Axes of the slice: x: 4 (x_hi: 2, x_lo: 2; x = x_hi * 2 + x_lo), y: 8, z: 8, core: 2. Of those that a mesh axis runs over, the one named last changes fastest.
Arguments:
- records: bfloat16 [4096, 26624], P('row', 'col'), may hold values from -400 to 400
- offsets: int32 [16], P('col'), may hold values from 0 to 164, as said below
- live_flags: int32 [4096], P('row'), may hold values 0 or 1
Outputs:
- cross_spectra: bfloat16 [32, 2, 4096, 4096], P('bin', None, 'row', 'col')
The draws below stay inside these ranges and needn't reach their ends.
Inputs may be any that keep to these rules, and one draw needn't show every extreme that they name: `offsets`: some window has delay 0 and some has delay 164.
All inputs are finite; a program needn't handle non-finite values. No bound on the sum of `live_flags` on one device may be relied on, other than what follows from the above.
Results may differ from the reference program's by a relative error of at most 0.007.
Values sent between devices are 32-bit elements; how exact they have to be, the bound alone decides.
A program may use at most 64 MiB of HBM per device.

```python
import math
import jax
import jax.numpy as jnp
from jax import lax

C = 4096
L = 1500
NB = 32
BSTEP = 6
SLACK = 164
WIN_DEV = 1
T_DEV = 1664
TIME = 26624
WINDOWS = 16


def draw_records(key, part):
    key = jax.random.fold_in(key, 11)
    key_noise, key_gain, key_common, key_weight = jax.random.split(key, 4)
    noise_field = jax.random.normal(key_noise, (C, TIME + 1), jnp.float32)
    channel_gain = jnp.exp(jax.random.uniform(key_gain, (C, 1), jnp.float32, 0.0, 2.3))
    shared_part = 0.3
    common = jnp.clip(jax.random.normal(key_common, (1, TIME), jnp.float32), -6.0, 6.0)
    weights = jax.random.uniform(key_weight, (C, 1), jnp.float32, 0.5, 1.5)
    colored = jnp.clip(noise_field[:, 1:], -6.0, 6.0) - 0.95 * jnp.clip(noise_field[:, :-1], -6.0, 6.0)
    return (channel_gain * (colored + shared_part * weights * common)).astype(jnp.bfloat16)


def draw_offsets(key, part):
    key = jax.random.fold_in(key, 5)
    key_values, key_low, key_high = jax.random.split(key, 3)
    values = jax.random.randint(key_values, (WINDOWS,), 0, SLACK + 1)
    low_slot = jax.random.randint(key_low, (), 0, WINDOWS)
    high_slot = (low_slot + 1 + jax.random.randint(key_high, (), 0, WINDOWS - 1)) % WINDOWS
    positions = lax.iota(jnp.int32, WINDOWS)
    values = jnp.where(positions == low_slot, 0, values)
    return jnp.where(positions == high_slot, SLACK, values).astype(jnp.int32)


def touch_ends(values, key, least, top_value):
    extent = values.shape
    spot = [jax.random.randint(jax.random.fold_in(key, axis), (), 0, extent[axis]) for axis in range(len(extent))]
    values = values.at[tuple(spot)].set(least)
    longest = extent.index(max(extent))
    spot[longest] = (spot[longest] + 1) % extent[longest]
    return values.at[tuple(spot)].set(top_value)


def setup_inputs(seed: int = 0) -> dict:
    arg_keys = jax.random.split(jax.random.key(seed), 4)
    records = draw_records(jax.random.fold_in(arg_keys[3], 71), 0)
    offsets = draw_offsets(jax.random.fold_in(arg_keys[3], 71), 0)
    live_flags = touch_ends((jax.random.randint(arg_keys[2], (C,), 0, 8) < 7).astype(jnp.int32), jax.random.fold_in(arg_keys[2], 1), 0, 1)
    return dict(records=records, offsets=offsets, live_flags=live_flags)


epsilon = 1e-05

def make_table(first_bin, bin_count, length, stride):
    bin_ids = (first_bin + lax.iota(jnp.int32, bin_count) + 1) * stride
    sample_ids = lax.iota(jnp.int32, length)
    angles = (bin_ids[:, None] * sample_ids[None, :] % length).astype(jnp.float32) * (2.0 * math.pi / length)
    tapering = 0.5 - 0.5 * jnp.cos(sample_ids.astype(jnp.float32) * (2.0 * math.pi / length))
    return jnp.stack([jnp.cos(angles) * tapering, -jnp.sin(angles) * tapering]).astype(jnp.bfloat16)

def reference(records, offsets, live_flags):
    dft_table = make_table(0, NB, L, BSTEP).reshape(2 * NB, L)

    def one_window(window_id):
        first_sample = window_id // WIN_DEV * T_DEV + window_id % WIN_DEV * L + offsets[window_id]
        segment = lax.dynamic_slice_in_dim(records, first_sample.astype(jnp.int32), L, 1)
        return jnp.dot(dft_table, segment.T, preferred_element_type=jnp.float32).reshape(2, NB, C)
    spectra = lax.map(one_window, lax.iota(jnp.int32, WINDOWS))
    energy = lax.optimization_barrier(jnp.sum(spectra * spectra, axis=(1, 2))) / (2 * NB)
    scaling = live_flags.astype(jnp.float32) / jnp.sqrt(energy + epsilon)
    whitened = spectra * scaling[:, None, None, :]
    highest = lax.Precision.HIGHEST

    def one_bin(bin_id):
        block = lax.dynamic_index_in_dim(whitened, bin_id, 2, keepdims=False)
        real_part = jnp.einsum('wpc,wpd->cd', block, block, precision=highest)
        imag_part = jnp.einsum('wc,wd->cd', block[:, 1], block[:, 0], precision=highest) - jnp.einsum('wc,wd->cd', block[:, 0], block[:, 1], precision=highest)
        return (jnp.stack([real_part, imag_part]) / WINDOWS).astype(jnp.bfloat16)
    return lax.map(one_bin, lax.iota(jnp.int32, NB))
```

```python
import math

import jax
import jax.numpy as jnp
import numpy as np
from jax import lax
from jax.experimental import pallas as pl
from jax.experimental.pallas import tpu as pltpu
from jax.sharding import PartitionSpec as P

L = 1500
NB = 32
BSTEP = 6
EPSILON = 1e-05
MESH = pl.DeviceIdType.MESH
SLOT = 64
WINDOWS = 16
NEAR_FIRST = (1, 7, 2, 6, 3, 5, 4)


def dft_rows():
    bins = (np.arange(NB) + 1) * BSTEP
    samples = np.arange(L)
    angles = (bins[:, None] * samples[None, :] % L) * (2.0 * math.pi / L)
    taper = 0.5 - 0.5 * np.cos(samples * (2.0 * math.pi / L))
    rows = np.stack([np.cos(angles) * taper, -np.sin(angles) * taper], axis=1)
    return jnp.asarray(rows.reshape(2 * NB, L).astype(np.float32)).astype(jnp.bfloat16)


def gather_kernel(spectra_ref, live_ref, left_ref, right_ref, send_sem, left_sem, right_sem):
    row, col, half = lax.axis_index("row"), lax.axis_index("col"), lax.axis_index("bin")
    y, core = row // 2, row % 2
    z, side = col // 2, col % 2

    def device(y, core, z, side):
        return (y * 2 + core, z * 2 + side, half)

    def along(step):
        return lax.rem(z + step, 8)

    barrier = pltpu.get_barrier_semaphore()
    partners = [device(y, core, along(i), side) for i in range(1, 8)]
    partners += [device(y, core, z, 1 - side), device(y, 1 - core, z, side)]
    for target in partners:
        pl.semaphore_signal(barrier, inc=1, device_id=target, device_id_type=MESH)
    for i in range(8):
        pl.semaphore_signal(
            barrier, inc=1, device_id=device(z, side, i, core), device_id_type=MESH
        )

    spectra = spectra_ref[...]
    energy = jnp.sum(spectra * spectra, axis=0, keepdims=True) / (2 * NB)
    scaling = live_ref[...].astype(jnp.float32) * lax.rsqrt(energy + EPSILON)
    mine = spectra_ref[pl.ds(pl.multiple_of(half * NB, NB), NB), :] * scaling
    left_ref[col, 0:32, :] = mine[:, :128]
    left_ref[col, 32:64, :] = mine[:, 128:]

    pl.semaphore_wait(barrier, 17)

    sent = []

    def send(source, target_ref, sem, device_id):
        copy = pltpu.make_async_remote_copy(
            src_ref=source,
            dst_ref=target_ref,
            send_sem=send_sem.at[len(sent)],
            recv_sem=sem,
            device_id=device_id,
            device_id_type=MESH,
        )
        sent.append(copy)
        return copy

    def wait_for(ref, sem, slot):
        pltpu.make_async_copy(ref.at[slot], ref.at[slot], sem.at[slot]).wait()

    own = left_ref.at[col]
    send(own, own, left_sem.at[col], device(y, core, z, 1 - side)).start()
    for i in NEAR_FIRST:
        send(own, own, left_sem.at[col], device(y, core, along(i), side)).start()
    for j in (1, 7, 2, 6, 3, 5, 4):
        send(
            own, right_ref.at[col], right_sem.at[col], device(lax.rem(y + j, 8), side, y, core)
        ).start()
    stays = jnp.logical_and(z == y, side == core)
    keep = pltpu.make_async_copy(own, right_ref.at[col], right_sem.at[col])
    move = send(own, right_ref.at[col], right_sem.at[col], device(y, side, y, core))

    @pl.when(stays)
    def _():
        keep.start()

    @pl.when(jnp.logical_not(stays))
    def _():
        move.start()

    for i in (0,) + NEAR_FIRST:
        if i:
            slot = along(i) * 2 + side
            wait_for(left_ref, left_sem, slot)
            block = left_ref.at[slot]
            send(block, block, left_sem.at[slot], device(y, core, z, 1 - side)).start()
        slot = along(i) * 2 + core
        wait_for(right_ref, right_sem, slot)
        block = right_ref.at[slot]
        send(block, block, right_sem.at[slot], device(y, 1 - core, z, side)).start()
    for i in (0,) + NEAR_FIRST:
        wait_for(left_ref, left_sem, along(i) * 2 + 1 - side)
        wait_for(right_ref, right_sem, along(i) * 2 + 1 - core)
    for copy in sent:
        if copy is not move:
            copy.wait_send()

    @pl.when(jnp.logical_not(stays))
    def _():
        move.wait_send()


def stack_kernel(left_ref, right_ref, out_ref):
    step = pl.program_id(0)
    for k in range(out_ref.shape[0]):
        first = (step * out_ref.shape[0] + k) * 2

        def rows(ref, part):
            return jnp.concatenate(
                [ref[pl.ds(first + part + h * 32, WINDOWS, stride=SLOT), :] for h in (0, 1)],
                axis=1,
            )

        real, imag = rows(right_ref, 0), rows(right_ref, 1)
        left = jnp.concatenate([rows(left_ref, 0), rows(left_ref, 1)], axis=0)
        left = left.astype(jnp.bfloat16)
        straight = jnp.concatenate([real, imag], axis=0).astype(jnp.bfloat16)
        turned = jnp.concatenate([-imag, real], axis=0).astype(jnp.bfloat16)
        for part, other in enumerate((straight, turned)):
            total = lax.dot_general(
                left, other, (((0,), (0,)), ((), ())), preferred_element_type=jnp.float32
            )
            out_ref[k, part] = (total * (1.0 / WINDOWS)).astype(out_ref.dtype)


def per_device(records, offsets, live_flags):
    segment = lax.dynamic_slice_in_dim(records, offsets[0], L, 1)
    spectra = lax.dot_general(
        dft_rows(), segment, (((1,), (1,)), ((), ())), preferred_element_type=jnp.float32
    )
    channels = records.shape[0]
    vmem = pl.BlockSpec(memory_space=pltpu.VMEM)
    gathered = jax.ShapeDtypeStruct((WINDOWS, SLOT, channels // 2), jnp.float32)
    left, right = pl.pallas_call(
        gather_kernel,
        out_shape=(gathered, gathered),
        in_specs=[vmem, vmem],
        out_specs=(vmem, vmem),
        scratch_shapes=[
            pltpu.SemaphoreType.DMA((31,)),
            pltpu.SemaphoreType.DMA((WINDOWS,)),
            pltpu.SemaphoreType.DMA((WINDOWS,)),
        ],
        compiler_params=pltpu.CompilerParams(
            collective_id=0, has_side_effects=True, vmem_limit_bytes=8 * 2**20
        ),
        name="gather_spectra",
    )(spectra, live_flags.reshape(1, channels))
    left = left.reshape(WINDOWS * SLOT, channels // 2)
    right = right.reshape(WINDOWS * SLOT, channels // 2)
    per_step = 4
    return pl.pallas_call(
        stack_kernel,
        grid=(16 // per_step,),
        out_shape=jax.ShapeDtypeStruct((16, 2, channels, channels), jnp.bfloat16),
        in_specs=[vmem, vmem],
        out_specs=pl.BlockSpec((per_step, 2, channels, channels), lambda i: (i, 0, 0, 0)),
        compiler_params=pltpu.CompilerParams(vmem_limit_bytes=16 * 2**20),
        name="stack_windows",
    )(left, right)


def solution(mesh):
    in_specs = (P("row", "col"), P("col"), P("row"))
    out_specs = P("bin", None, "row", "col")
    return jax.shard_map(
        per_device, mesh=mesh, in_specs=in_specs, out_specs=out_specs, check_vma=False
    )
```

```python
import math

import jax
import jax.numpy as jnp
import numpy as np
from jax import lax
from jax.experimental import pallas as pl
from jax.experimental.pallas import tpu as pltpu
from jax.sharding import PartitionSpec as P

L = 1500
NB = 32
BSTEP = 6
EPSILON = 1e-05
MESH = pl.DeviceIdType.MESH
SLOT = 64
WINDOWS = 16
NEAR_FIRST = (1, 7, 2, 6, 3, 5, 4)


def dft_rows(samples_held):
    bins = (np.arange(NB) + 1) * BSTEP
    samples = np.arange(L)
    angles = (bins[:, None] * samples[None, :] % L) * (2.0 * math.pi / L)
    taper = 0.5 - 0.5 * np.cos(samples * (2.0 * math.pi / L))
    rows = np.stack([np.cos(angles) * taper, -np.sin(angles) * taper], axis=1)
    rows = jnp.asarray(rows.reshape(2 * NB, L).astype(np.float32)).astype(jnp.bfloat16)
    return jnp.pad(rows.astype(jnp.float32), ((0, 0), (0, samples_held - L)))


def gather_kernel(
    records_hbm, table_hbm, offsets_hbm, live_hbm, left_ref, right_ref,
    records_ref, table_ref, offsets_ref, live_ref, load_sem, send_sem, left_sem, right_sem,
):
    row, col, half = lax.axis_index("row"), lax.axis_index("col"), lax.axis_index("bin")
    y, core = row // 2, row % 2
    z, side = col // 2, col % 2

    def device(y, core, z, side):
        return (y * 2 + core, z * 2 + side, half)

    def up(step):
        return lax.rem(y + step, 8)

    def along(step):
        return lax.rem(z + step, 8)

    parity = lax.rem(y + z, 2)
    diagonal = jnp.logical_and(z == y, side == core)

    barrier = pltpu.get_barrier_semaphore()

    def greet(target):
        pl.semaphore_signal(barrier, inc=1, device_id=target, device_id_type=MESH)

    for i in NEAR_FIRST:
        greet(device(y, core, along(i), side))
    greet(device(y, core, z, 1 - side))
    greet(device(y, 1 - core, z, side))
    for step in (1, 7):
        for k in range(2):
            greet(device(up(step), k, z, side))
    for i in range(4):
        source = parity + 2 * i
        own_window = jnp.logical_and(diagonal, source == z)
        pl.when(jnp.logical_not(own_window))(
            lambda source=source: greet(device(z, side, source, core))
        )

    loads = [
        pltpu.make_async_copy(source, target, load_sem.at[i])
        for i, (source, target) in enumerate(
            (
                (offsets_hbm, offsets_ref),
                (table_hbm, table_ref),
                (records_hbm, records_ref),
                (live_hbm, live_ref),
            )
        )
    ]
    for load in loads:
        load.start()
    for load in loads:
        load.wait()
    table = pltpu.roll(table_ref[...], offsets_ref[0], 1).astype(jnp.bfloat16)
    spectra = lax.dot_general(
        table, records_ref[...], (((1,), (1,)), ((), ())), preferred_element_type=jnp.float32
    )
    energy = jnp.sum(spectra * spectra, axis=0, keepdims=True) / (2 * NB)
    scaling = live_ref[...].astype(jnp.float32) * lax.rsqrt(energy + EPSILON)
    whitened = spectra * scaling
    mine = jnp.where(half == 0, whitened[:NB], whitened[NB:])
    left_ref[col, 0:32, :] = mine[:, :128]
    left_ref[col, 32:64, :] = mine[:, 128:]

    self_sends = jnp.logical_and(diagonal, parity == lax.rem(y, 2))
    pl.semaphore_wait(barrier, 17 - self_sends.astype(jnp.int32))

    sent = []

    def send(source, target_ref, sem, device_id):
        copy = pltpu.make_async_remote_copy(
            src_ref=source,
            dst_ref=target_ref,
            send_sem=send_sem.at[len(sent)],
            recv_sem=sem,
            device_id=device_id,
            device_id_type=MESH,
        )
        sent.append(copy)
        return copy

    def wait_for(ref, sem, slot):
        pltpu.make_async_copy(ref.at[slot], ref.at[slot], sem.at[slot]).wait()

    own = left_ref.at[col]
    send(own, own, left_sem.at[col], device(y, core, z, 1 - side)).start()
    for i in NEAR_FIRST:
        send(own, own, left_sem.at[col], device(y, core, along(i), side)).start()
    keep = pltpu.make_async_copy(own, right_ref.at[col], right_sem.at[col])
    moves = []
    for i in range(4):
        target = parity + 2 * i
        stays = jnp.logical_and(diagonal, target == y)
        move = send(own, right_ref.at[col], right_sem.at[col], device(target, side, y, core))
        pl.when(stays)(keep.start)
        pl.when(jnp.logical_not(stays))(move.start)
        moves.append((move, stays))

    def hand_left(i):
        slot = along(i) * 2 + side
        wait_for(left_ref, left_sem, slot)
        block = left_ref.at[slot]
        send(block, block, left_sem.at[slot], device(y, core, z, 1 - side)).start()

    def hand_right(i):
        slot = (parity + 2 * i) * 2 + core
        wait_for(right_ref, right_sem, slot)
        block = right_ref.at[slot]
        for k in range(2):
            send(block, block, right_sem.at[slot], device(up((1, 7)[i % 2]), k, z, side)).start()
        send(block, block, right_sem.at[slot], device(y, 1 - core, z, side)).start()

    for n, i in enumerate(NEAR_FIRST):
        hand_left(i)
        if 2 <= n < 6:
            hand_right(n - 2)
    for i in (0,) + NEAR_FIRST:
        wait_for(left_ref, left_sem, along(i) * 2 + 1 - side)
    for i in range(8):
        pl.when(parity != i % 2)(
            lambda i=i: wait_for(right_ref, right_sem, i * 2 + core)
        )
        wait_for(right_ref, right_sem, i * 2 + 1 - core)
    staying = [move for move, _ in moves]
    for copy in sent:
        if not any(copy is move for move in staying):
            copy.wait_send()
    for move, stays in moves:
        pl.when(jnp.logical_not(stays))(move.wait_send)


def stack_kernel(left_ref, right_ref, out_ref):
    step = pl.program_id(0)
    for k in range(out_ref.shape[0]):
        first = (step * out_ref.shape[0] + k) * 2

        def rows(ref, part):
            return jnp.concatenate(
                [ref[pl.ds(first + part + h * 32, WINDOWS, stride=SLOT), :] for h in (0, 1)],
                axis=1,
            )

        real, imag = rows(right_ref, 0), rows(right_ref, 1)
        left = jnp.concatenate([rows(left_ref, 0), rows(left_ref, 1)], axis=0)
        left = left.astype(jnp.bfloat16)
        straight = jnp.concatenate([real, imag], axis=0).astype(jnp.bfloat16)
        turned = jnp.concatenate([-imag, real], axis=0).astype(jnp.bfloat16)
        for part, other in enumerate((straight, turned)):
            total = lax.dot_general(
                left, other, (((0,), (0,)), ((), ())), preferred_element_type=jnp.float32
            )
            out_ref[k, part] = (total * (1.0 / WINDOWS)).astype(out_ref.dtype)


def per_device(records, offsets, live_flags):
    channels, held = records.shape
    vmem = pl.BlockSpec(memory_space=pltpu.VMEM)
    hbm = pl.BlockSpec(memory_space=pltpu.HBM)
    gathered = jax.ShapeDtypeStruct((WINDOWS, SLOT, channels // 2), jnp.float32)
    left, right = pl.pallas_call(
        gather_kernel,
        out_shape=(gathered, gathered),
        in_specs=[hbm] * 4,
        out_specs=(vmem, vmem),
        scratch_shapes=[
            pltpu.VMEM((channels, held), jnp.bfloat16),
            pltpu.VMEM((2 * NB, held), jnp.float32),
            pltpu.SMEM((1,), jnp.int32),
            pltpu.VMEM((1, channels), jnp.int32),
            pltpu.SemaphoreType.DMA((4,)),
            pltpu.SemaphoreType.DMA((31,)),
            pltpu.SemaphoreType.DMA((WINDOWS,)),
            pltpu.SemaphoreType.DMA((WINDOWS,)),
        ],
        compiler_params=pltpu.CompilerParams(
            collective_id=0, has_side_effects=True, vmem_limit_bytes=52 * 2**20
        ),
        name="gather_spectra",
    )(records, dft_rows(held), offsets, live_flags.reshape(1, channels))
    left = left.reshape(WINDOWS * SLOT, channels // 2)
    right = right.reshape(WINDOWS * SLOT, channels // 2)
    per_step = 4
    return pl.pallas_call(
        stack_kernel,
        grid=(16 // per_step,),
        out_shape=jax.ShapeDtypeStruct((16, 2, channels, channels), jnp.bfloat16),
        in_specs=[vmem, vmem],
        out_specs=pl.BlockSpec((per_step, 2, channels, channels), lambda i: (i, 0, 0, 0)),
        compiler_params=pltpu.CompilerParams(vmem_limit_bytes=16 * 2**20),
        name="stack_windows",
    )(left, right)


def solution(mesh):
    in_specs = (P("row", "col"), P("col"), P("row"))
    out_specs = P("bin", None, "row", "col")
    return jax.shard_map(
        per_device, mesh=mesh, in_specs=in_specs, out_specs=out_specs, check_vma=False
    )
```

```python
import math

import jax
import jax.numpy as jnp
import numpy as np
from jax import lax
from jax.experimental import pallas as pl
from jax.experimental.pallas import tpu as pltpu
from jax.sharding import PartitionSpec as P

L = 1500
NB = 32
BSTEP = 6
EPSILON = 1e-05
MESH = pl.DeviceIdType.MESH
SLOT = 64
WINDOWS = 16
NEAR_FIRST = (1, 7, 2, 6, 3, 5, 4)


def dft_rows(samples_held):
    bins = (np.arange(NB) + 1) * BSTEP
    samples = np.arange(L)
    angles = (bins[:, None] * samples[None, :] % L) * (2.0 * math.pi / L)
    taper = 0.5 - 0.5 * np.cos(samples * (2.0 * math.pi / L))
    rows = np.stack([np.cos(angles) * taper, -np.sin(angles) * taper], axis=1)
    rows = jnp.asarray(rows.reshape(2 * NB, L).astype(np.float32)).astype(jnp.bfloat16)
    return jnp.pad(rows.astype(jnp.float32), ((0, 0), (0, samples_held - L)))


def gather_kernel(
    records_hbm, table_hbm, offsets_hbm, live_hbm, left_ref, right_ref,
    records_ref, table_ref, offsets_ref, live_ref, load_sem, send_sem, left_sem, right_sem,
):
    row, col, half = lax.axis_index("row"), lax.axis_index("col"), lax.axis_index("bin")
    y, core = row // 2, row % 2
    z, side = col // 2, col % 2

    def device(y, core, z, side):
        return (y * 2 + core, z * 2 + side, half)

    def up(step):
        return lax.rem(y + step, 8)

    def along(step):
        return lax.rem(z + step, 8)

    parity = lax.rem(y + z, 2)
    diagonal = jnp.logical_and(z == y, side == core)

    barrier = pltpu.get_barrier_semaphore()

    def greet(target):
        pl.semaphore_signal(barrier, inc=1, device_id=target, device_id_type=MESH)

    for i in NEAR_FIRST:
        greet(device(y, core, along(i), side))
    greet(device(y, core, z, 1 - side))
    greet(device(y, 1 - core, z, side))
    for step in (1, 7):
        for k in range(2):
            greet(device(up(step), k, z, side))
    for i in range(4):
        source = parity + 2 * i
        own_window = jnp.logical_and(diagonal, source == z)
        pl.when(jnp.logical_not(own_window))(
            lambda source=source: greet(device(z, side, source, core))
        )

    loads = [
        pltpu.make_async_copy(source, target, load_sem.at[i])
        for i, (source, target) in enumerate(
            (
                (offsets_hbm, offsets_ref),
                (table_hbm, table_ref),
                (records_hbm, records_ref),
                (live_hbm, live_ref),
            )
        )
    ]
    for load in loads:
        load.start()
    for load in loads:
        load.wait()
    table = pltpu.roll(table_ref[...], offsets_ref[0], 1).astype(jnp.bfloat16)
    spectra = lax.dot_general(
        table, records_ref[...], (((1,), (1,)), ((), ())), preferred_element_type=jnp.float32
    )
    energy = jnp.sum(spectra * spectra, axis=0, keepdims=True) / (2 * NB)
    scaling = live_ref[...].astype(jnp.float32) * lax.rsqrt(energy + EPSILON)
    whitened = spectra * scaling
    mine = jnp.where(half == 0, whitened[:NB], whitened[NB:])
    left_ref[col, 0:32, :] = mine[:, :128]
    left_ref[col, 32:64, :] = mine[:, 128:]

    self_sends = jnp.logical_and(diagonal, parity == lax.rem(y, 2))
    pl.semaphore_wait(barrier, 17 - self_sends.astype(jnp.int32))

    sent = []

    def send(source, target_ref, sem, device_id):
        copy = pltpu.make_async_remote_copy(
            src_ref=source,
            dst_ref=target_ref,
            send_sem=send_sem.at[len(sent)],
            recv_sem=sem,
            device_id=device_id,
            device_id_type=MESH,
        )
        sent.append(copy)
        return copy

    def wait_for(ref, sem, slot):
        pltpu.make_async_copy(ref.at[slot], ref.at[slot], sem.at[slot]).wait()

    own = left_ref.at[col]
    send(own, own, left_sem.at[col], device(y, core, z, 1 - side)).start()
    for i in NEAR_FIRST:
        send(own, own, left_sem.at[col], device(y, core, along(i), side)).start()
    keep = pltpu.make_async_copy(own, right_ref.at[col], right_sem.at[col])
    moves = []
    for i in range(4):
        target = parity + 2 * i
        stays = jnp.logical_and(diagonal, target == y)
        move = send(own, right_ref.at[col], right_sem.at[col], device(target, side, y, core))
        pl.when(stays)(keep.start)
        pl.when(jnp.logical_not(stays))(move.start)
        moves.append((move, stays))

    def hand_left(i):
        slot = along(i) * 2 + side
        wait_for(left_ref, left_sem, slot)
        block = left_ref.at[slot]
        send(block, block, left_sem.at[slot], device(y, core, z, 1 - side)).start()

    def hand_right(i):
        slot = (parity + 2 * i) * 2 + core
        wait_for(right_ref, right_sem, slot)
        block = right_ref.at[slot]
        for k in range(2):
            send(block, block, right_sem.at[slot], device(up((1, 7)[i % 2]), k, z, side)).start()
        send(block, block, right_sem.at[slot], device(y, 1 - core, z, side)).start()

    for n, i in enumerate(NEAR_FIRST):
        hand_left(i)
        if 2 <= n < 6:
            hand_right(n - 2)
    for i in (0,) + NEAR_FIRST:
        wait_for(left_ref, left_sem, along(i) * 2 + 1 - side)
    for i in range(8):
        pl.when(parity != i % 2)(
            lambda i=i: wait_for(right_ref, right_sem, i * 2 + core)
        )
        wait_for(right_ref, right_sem, i * 2 + 1 - core)
    staying = [move for move, _ in moves]
    for copy in sent:
        if not any(copy is move for move in staying):
            copy.wait_send()
    for move, stays in moves:
        pl.when(jnp.logical_not(stays))(move.wait_send)


def stack_kernel(left_ref, right_ref, out_hbm, ready_ref, store_sem):
    def store(first):
        block = pl.ds(first, 2)
        return pltpu.make_async_copy(
            ready_ref.at[block], out_hbm.at[block], store_sem.at[first // 2]
        )

    def rows(ref, f, part):
        return jnp.concatenate(
            [ref[pl.ds(2 * f + part + h * 32, WINDOWS, stride=SLOT), :] for h in (0, 1)], axis=1
        )

    def stack(f):
        left = jnp.concatenate([rows(left_ref, f, 0), rows(left_ref, f, 1)], axis=0)
        left = (left * (1.0 / WINDOWS)).astype(jnp.bfloat16)
        real, imag = rows(right_ref, f, 0), rows(right_ref, f, 1)
        straight = jnp.concatenate([real, imag], axis=0).astype(jnp.bfloat16)
        turned = jnp.concatenate([-imag, real], axis=0).astype(jnp.bfloat16)
        for part, other in enumerate((straight, turned)):
            total = lax.dot_general(
                left, other, (((0,), (0,)), ((), ())), preferred_element_type=jnp.float32
            )
            ready_ref[f, part] = total.astype(ready_ref.dtype)

    for f in range(16):
        stack(f)
        if f % 2 == 2 - 1:
            store(f + 1 - 2).start()
    for first in range(0, 16, 2):
        store(first).wait()


def per_device(records, offsets, live_flags):
    channels, held = records.shape
    vmem = pl.BlockSpec(memory_space=pltpu.VMEM)
    hbm = pl.BlockSpec(memory_space=pltpu.HBM)
    gathered = jax.ShapeDtypeStruct((WINDOWS, SLOT, channels // 2), jnp.float32)
    left, right = pl.pallas_call(
        gather_kernel,
        out_shape=(gathered, gathered),
        in_specs=[hbm] * 4,
        out_specs=(vmem, vmem),
        scratch_shapes=[
            pltpu.VMEM((channels, held), jnp.bfloat16),
            pltpu.VMEM((2 * NB, held), jnp.float32),
            pltpu.SMEM((1,), jnp.int32),
            pltpu.VMEM((1, channels), jnp.int32),
            pltpu.SemaphoreType.DMA((4,)),
            pltpu.SemaphoreType.DMA((31,)),
            pltpu.SemaphoreType.DMA((WINDOWS,)),
            pltpu.SemaphoreType.DMA((WINDOWS,)),
        ],
        compiler_params=pltpu.CompilerParams(
            collective_id=0, has_side_effects=True, vmem_limit_bytes=12 * 2**20
        ),
        name="gather_spectra",
    )(
        pltpu.with_memory_space_constraint(records, pltpu.HBM),
        pltpu.with_memory_space_constraint(dft_rows(held), pltpu.HBM),
        offsets,
        pltpu.with_memory_space_constraint(live_flags.reshape(1, channels), pltpu.HBM),
    )
    left = left.reshape(WINDOWS * SLOT, channels // 2)
    right = right.reshape(WINDOWS * SLOT, channels // 2)
    shape = (16, 2, channels, channels)
    return pl.pallas_call(
        stack_kernel,
        out_shape=jax.ShapeDtypeStruct(shape, jnp.bfloat16),
        in_specs=[vmem, vmem],
        out_specs=pl.BlockSpec(memory_space=pltpu.HBM),
        scratch_shapes=[
            pltpu.VMEM(shape, jnp.bfloat16),
            pltpu.SemaphoreType.DMA((8,)),
        ],
        compiler_params=pltpu.CompilerParams(vmem_limit_bytes=16 * 2**20),
        name="stack_windows",
    )(left, right)


def solution(mesh):
    in_specs = (P("row", "col"), P("col"), P("row"))
    out_specs = P("bin", None, "row", "col")
    return jax.shard_map(
        per_device, mesh=mesh, in_specs=in_specs, out_specs=out_specs, check_vma=False
    )
```

```python
import math

import jax
import jax.numpy as jnp
import numpy as np
from jax import lax
from jax.experimental import pallas as pl
from jax.experimental.pallas import tpu as pltpu
from jax.sharding import PartitionSpec as P

L = 1500
NB = 32
BSTEP = 6
EPSILON = 1e-05
MESH = pl.DeviceIdType.MESH
SLOT = 64
WINDOWS = 16
NEAR_FIRST = (1, 7, 2, 6, 3, 5, 4)


def dft_rows(samples_held):
    bins = (np.arange(NB) + 1) * BSTEP
    samples = np.arange(L)
    angles = (bins[:, None] * samples[None, :] % L) * (2.0 * math.pi / L)
    taper = 0.5 - 0.5 * np.cos(samples * (2.0 * math.pi / L))
    rows = np.stack([np.cos(angles) * taper, -np.sin(angles) * taper], axis=1)
    rows = jnp.asarray(rows.reshape(2 * NB, L).astype(np.float32)).astype(jnp.bfloat16)
    return jnp.pad(rows.astype(jnp.float32), ((0, 0), (0, samples_held - L)))


def gather_kernel(
    records_hbm, table_hbm, offsets_hbm, live_hbm, left_ref, right_ref,
    records_ref, table_ref, offsets_ref, live_ref, load_sem, send_sem, left_sem, right_sem, opposite_sem,
):
    row, col, half = lax.axis_index("row"), lax.axis_index("col"), lax.axis_index("bin")
    y, core = row // 2, row % 2
    z, side = col // 2, col % 2

    def device(y, core, z, side):
        return (y * 2 + core, z * 2 + side, half)

    def up(step):
        return lax.rem(y + step, 8)

    def along(step):
        return lax.rem(z + step, 8)

    parity = lax.rem(y + z, 2)
    diagonal = jnp.logical_and(z == y, side == core)

    barrier = pltpu.get_barrier_semaphore()

    def greet(target):
        pl.semaphore_signal(barrier, inc=1, device_id=target, device_id_type=MESH)

    for i in NEAR_FIRST:
        greet(device(y, core, along(i), side))
    greet(device(y, core, z, 1 - side))
    greet(device(y, 1 - core, z, side))
    for step in (1, 7):
        for k in range(2):
            greet(device(up(step), k, z, side))
    for i in range(4):
        source = parity + 2 * i
        own_window = jnp.logical_and(diagonal, source == z)
        pl.when(jnp.logical_not(own_window))(
            lambda source=source: greet(device(z, side, source, core))
        )

    loads = [
        pltpu.make_async_copy(source, target, load_sem.at[i])
        for i, (source, target) in enumerate(
            (
                (offsets_hbm, offsets_ref),
                (table_hbm, table_ref),
                (records_hbm, records_ref),
                (live_hbm, live_ref),
            )
        )
    ]
    for load in loads:
        load.start()
    for load in loads:
        load.wait()
    table = pltpu.roll(table_ref[...], offsets_ref[0], 1).astype(jnp.bfloat16)
    spectra = lax.dot_general(
        table, records_ref[...], (((1,), (1,)), ((), ())), preferred_element_type=jnp.float32
    )
    energy = jnp.sum(spectra * spectra, axis=0, keepdims=True) / (2 * NB)
    scaling = live_ref[...].astype(jnp.float32) * lax.rsqrt(energy + EPSILON)
    whitened = spectra * scaling
    mine = jnp.where(half == 0, whitened[:NB], whitened[NB:])
    left_ref[col, 0:32, :] = mine[:, :128]
    left_ref[col, 32:64, :] = mine[:, 128:]

    self_sends = jnp.logical_and(diagonal, parity == lax.rem(y, 2))
    pl.semaphore_wait(barrier, 17 - self_sends.astype(jnp.int32))

    sent = []

    def send(source, target_ref, sem, device_id):
        copy = pltpu.make_async_remote_copy(
            src_ref=source,
            dst_ref=target_ref,
            send_sem=send_sem.at[len(sent)],
            recv_sem=sem,
            device_id=device_id,
            device_id_type=MESH,
        )
        sent.append(copy)
        return copy

    def wait_for(ref, sem, slot):
        pltpu.make_async_copy(ref.at[slot], ref.at[slot], sem.at[slot]).wait()

    own = left_ref.at[col]
    send(own, own, left_sem.at[col], device(y, core, z, 1 - side)).start()
    for i in (1, 7, 3, 5, 2, 6):
        send(own, own, left_sem.at[col], device(y, core, along(i), side)).start()
    keep = pltpu.make_async_copy(own, right_ref.at[col], right_sem.at[col])
    moves = []
    for i in range(4):
        target = parity + 2 * i
        stays = jnp.logical_and(diagonal, target == y)
        move = send(own, right_ref.at[col], right_sem.at[col], device(target, side, y, core))
        pl.when(stays)(keep.start)
        pl.when(jnp.logical_not(stays))(move.start)
        moves.append((move, stays))

    lefts, rights = {}, {}
    for i in NEAR_FIRST:
        slot = along(i) * 2 + side
        block = left_ref.at[slot]
        lefts[i] = slot, send(block, block, left_sem.at[slot], device(y, core, z, 1 - side))
    for i in range(4):
        slot = (parity + 2 * i) * 2 + core
        block = right_ref.at[slot]
        onward = [
            send(block, block, right_sem.at[slot], device(up((1, 7)[i % 2]), k, z, side))
            for k in range(2)
        ]
        onward.append(send(block, block, right_sem.at[slot], device(y, 1 - core, z, side)))
        rights[i] = slot, onward

    def opposite(i):
        slot = along(i) * 2 + side
        block = left_ref.at[slot]
        return pltpu.make_async_remote_copy(
            src_ref=block,
            dst_ref=block,
            send_sem=opposite_sem,
            recv_sem=left_sem.at[slot],
            device_id=device(y, core, along(7 if i == 3 else 1), side),
            device_id_type=MESH,
        )

    def hand_left(i):
        slot, copy = lefts[i]
        wait_for(left_ref, left_sem, slot)
        if i in (3, 5):
            pl.when(core == (i == 3))(opposite(i).start)
        copy.start()

    def hand_right(i):
        slot, onward = rights[i]
        wait_for(right_ref, right_sem, slot)
        for copy in onward:
            copy.start()

    def hand_on(order):
        for name in order.split():
            (hand_left if name[0] == "L" else hand_right)(int(name[1]))

    hand_on("L1 L7 L5 L3 R0 L2 R1 L6 R2 L4 R3")
    for i in (0,) + NEAR_FIRST:
        wait_for(left_ref, left_sem, along(i) * 2 + 1 - side)
    for i in range(8):
        pl.when(parity != i % 2)(
            lambda i=i: wait_for(right_ref, right_sem, i * 2 + core)
        )
        wait_for(right_ref, right_sem, i * 2 + 1 - core)
    staying = [move for move, _ in moves]
    for copy in sent:
        if not any(copy is move for move in staying):
            copy.wait_send()
    for move, stays in moves:
        pl.when(jnp.logical_not(stays))(move.wait_send)
    opposite(3).wait_send()


def stack_kernel(left_ref, right_ref, out_hbm, ready_ref, store_sem):
    def store(first):
        block = pl.ds(first, 2)
        return pltpu.make_async_copy(
            ready_ref.at[block], out_hbm.at[block], store_sem.at[first // 2]
        )

    def rows(ref, f, part):
        return jnp.concatenate(
            [ref[pl.ds(2 * f + part + h * 32, WINDOWS, stride=SLOT), :] for h in (0, 1)], axis=1
        )

    def stack(f):
        left = jnp.concatenate([rows(left_ref, f, 0), rows(left_ref, f, 1)], axis=0)
        left = (left * (1.0 / WINDOWS)).astype(jnp.bfloat16)
        real, imag = rows(right_ref, f, 0), rows(right_ref, f, 1)
        straight = jnp.concatenate([real, imag], axis=0).astype(jnp.bfloat16)
        turned = jnp.concatenate([-imag, real], axis=0).astype(jnp.bfloat16)
        for part, other in enumerate((straight, turned)):
            total = lax.dot_general(
                left, other, (((0,), (0,)), ((), ())), preferred_element_type=jnp.float32
            )
            ready_ref[f, part] = total.astype(ready_ref.dtype)

    for f in range(16):
        stack(f)
        if f % 2 == 2 - 1:
            store(f + 1 - 2).start()
    for first in range(0, 16, 2):
        store(first).wait()


def per_device(records, offsets, live_flags):
    channels, held = records.shape
    vmem = pl.BlockSpec(memory_space=pltpu.VMEM)
    hbm = pl.BlockSpec(memory_space=pltpu.HBM)
    gathered = jax.ShapeDtypeStruct((WINDOWS, SLOT, channels // 2), jnp.float32)
    left, right = pl.pallas_call(
        gather_kernel,
        out_shape=(gathered, gathered),
        in_specs=[hbm] * 4,
        out_specs=(vmem, vmem),
        scratch_shapes=[
            pltpu.VMEM((channels, held), jnp.bfloat16),
            pltpu.VMEM((2 * NB, held), jnp.float32),
            pltpu.SMEM((1,), jnp.int32),
            pltpu.VMEM((1, channels), jnp.int32),
            pltpu.SemaphoreType.DMA((4,)),
            pltpu.SemaphoreType.DMA((31,)),
            pltpu.SemaphoreType.DMA((WINDOWS,)),
            pltpu.SemaphoreType.DMA((WINDOWS,)),
            pltpu.SemaphoreType.DMA,
        ],
        compiler_params=pltpu.CompilerParams(
            collective_id=0, has_side_effects=True, vmem_limit_bytes=12 * 2**20
        ),
        name="gather_spectra",
    )(
        pltpu.with_memory_space_constraint(records, pltpu.HBM),
        pltpu.with_memory_space_constraint(dft_rows(held), pltpu.HBM),
        offsets,
        pltpu.with_memory_space_constraint(live_flags.reshape(1, channels), pltpu.HBM),
    )
    left = left.reshape(WINDOWS * SLOT, channels // 2)
    right = right.reshape(WINDOWS * SLOT, channels // 2)
    shape = (16, 2, channels, channels)
    return pl.pallas_call(
        stack_kernel,
        out_shape=jax.ShapeDtypeStruct(shape, jnp.bfloat16),
        in_specs=[vmem, vmem],
        out_specs=pl.BlockSpec(memory_space=pltpu.HBM),
        scratch_shapes=[
            pltpu.VMEM(shape, jnp.bfloat16),
            pltpu.SemaphoreType.DMA((8,)),
        ],
        compiler_params=pltpu.CompilerParams(vmem_limit_bytes=16 * 2**20),
        name="stack_windows",
    )(left, right)


def solution(mesh):
    in_specs = (P("row", "col"), P("col"), P("row"))
    out_specs = P("bin", None, "row", "col")
    return jax.shard_map(
        per_device, mesh=mesh, in_specs=in_specs, out_specs=out_specs, check_vma=False
    )
```

```python
import math

import jax
import jax.numpy as jnp
import numpy as np
from jax import lax
from jax.experimental import pallas as pl
from jax.experimental.pallas import tpu as pltpu
from jax.sharding import PartitionSpec as P

L = 1500
NB = 32
BSTEP = 6
EPSILON = 1e-05
MESH = pl.DeviceIdType.MESH
SLOT = 64
WINDOWS = 16
NEAR_FIRST = (1, 7, 2, 6, 3, 5, 4)


def dft_rows(samples_held):
    bins = (np.arange(NB) + 1) * BSTEP
    samples = np.arange(L)
    angles = (bins[:, None] * samples[None, :] % L) * (2.0 * math.pi / L)
    taper = 0.5 - 0.5 * np.cos(samples * (2.0 * math.pi / L))
    rows = np.stack([np.cos(angles) * taper, -np.sin(angles) * taper], axis=1)
    rows = jnp.asarray(rows.reshape(2 * NB, L).astype(np.float32)).astype(jnp.bfloat16)
    return jnp.pad(rows.astype(jnp.float32), ((0, 0), (0, samples_held - L)))


def gather_kernel(
    records_hbm, table_hbm, offsets_hbm, live_hbm, left_ref, right_ref,
    records_ref, table_ref, offsets_ref, live_ref, load_sem, send_sem, left_sem, right_sem, opposite_sem,
):
    row, col, half = lax.axis_index("row"), lax.axis_index("col"), lax.axis_index("bin")
    y, core = row // 2, row % 2
    z, side = col // 2, col % 2

    def device(y, core, z, side):
        return (y * 2 + core, z * 2 + side, half)

    def up(step):
        return lax.rem(y + step, 8)

    def along(step):
        return lax.rem(z + step, 8)

    parity = lax.rem(y + z, 2)
    diagonal = jnp.logical_and(z == y, side == core)

    barrier = pltpu.get_barrier_semaphore()

    def greet(target):
        pl.semaphore_signal(barrier, inc=1, device_id=target, device_id_type=MESH)

    for i in NEAR_FIRST:
        greet(device(y, core, along(i), side))
    greet(device(y, core, z, 1 - side))
    greet(device(y, 1 - core, z, side))
    for step in (1, 7):
        for k in range(2):
            greet(device(up(step), k, z, side))
    for i in range(4):
        source = parity + 2 * i
        own_window = jnp.logical_and(diagonal, source == z)
        pl.when(jnp.logical_not(own_window))(
            lambda source=source: greet(device(z, side, source, core))
        )

    loads = [
        pltpu.make_async_copy(source, target, load_sem.at[i])
        for i, (source, target) in enumerate(
            (
                (offsets_hbm, offsets_ref),
                (table_hbm, table_ref),
                (records_hbm, records_ref),
                (live_hbm, live_ref),
            )
        )
    ]
    for load in loads:
        load.start()
    for load in loads:
        load.wait()
    table = pltpu.roll(table_ref[...], offsets_ref[0], 1).astype(jnp.bfloat16)
    spectra = lax.dot_general(
        table, records_ref[...], (((1,), (1,)), ((), ())), preferred_element_type=jnp.float32
    )
    energy = jnp.sum(spectra * spectra, axis=0, keepdims=True) / (2 * NB)
    scaling = live_ref[...].astype(jnp.float32) * lax.rsqrt(energy + EPSILON)
    whitened = spectra * scaling
    mine = jnp.where(half == 0, whitened[:NB], whitened[NB:])
    left_ref[col, 0:32, :] = mine[:, :128]
    left_ref[col, 32:64, :] = mine[:, 128:]

    self_sends = jnp.logical_and(diagonal, parity == lax.rem(y, 2))
    pl.semaphore_wait(barrier, 17 - self_sends.astype(jnp.int32))

    sent = []

    def send(source, target_ref, sem, device_id):
        copy = pltpu.make_async_remote_copy(
            src_ref=source,
            dst_ref=target_ref,
            send_sem=send_sem.at[len(sent)],
            recv_sem=sem,
            device_id=device_id,
            device_id_type=MESH,
        )
        sent.append(copy)
        return copy

    def wait_for(ref, sem, slot):
        pltpu.make_async_copy(ref.at[slot], ref.at[slot], sem.at[slot]).wait()

    own = left_ref.at[col]
    keep = pltpu.make_async_copy(own, right_ref.at[col], right_sem.at[col])
    moves = []
    for i in range(4):
        target = parity + 2 * i
        stays = jnp.logical_and(diagonal, target == y)
        move = send(own, right_ref.at[col], right_sem.at[col], device(target, side, y, core))
        pl.when(stays)(keep.start)
        pl.when(jnp.logical_not(stays))(move.start)
        moves.append((move, stays))

    send(own, own, left_sem.at[col], device(y, core, z, 1 - side)).start()
    for i in (1, 7, 3, 5, 2, 6):
        send(own, own, left_sem.at[col], device(y, core, along(i), side)).start()
    lefts, rights = {}, {}
    for i in NEAR_FIRST:
        slot = along(i) * 2 + side
        block = left_ref.at[slot]
        lefts[i] = slot, send(block, block, left_sem.at[slot], device(y, core, z, 1 - side))
    for i in range(4):
        slot = (parity + 2 * i) * 2 + core
        block = right_ref.at[slot]
        onward = [
            send(block, block, right_sem.at[slot], device(up((1, 7)[i % 2]), k, z, side))
            for k in range(2)
        ]
        onward.append(send(block, block, right_sem.at[slot], device(y, 1 - core, z, side)))
        rights[i] = slot, onward

    def opposite(i):
        slot = along(i) * 2 + side
        block = left_ref.at[slot]
        return pltpu.make_async_remote_copy(
            src_ref=block,
            dst_ref=block,
            send_sem=opposite_sem,
            recv_sem=left_sem.at[slot],
            device_id=device(y, core, along(7 if i == 3 else 1), side),
            device_id_type=MESH,
        )

    def hand_left(i):
        slot, copy = lefts[i]
        wait_for(left_ref, left_sem, slot)
        if i in (3, 5):
            pl.when(core == (i == 3))(opposite(i).start)
        copy.start()

    def hand_right(i):
        slot, onward = rights[i]
        wait_for(right_ref, right_sem, slot)
        for copy in onward:
            copy.start()

    def hand_on(order):
        for name in order.split():
            (hand_left if name[0] == "L" else hand_right)(int(name[1]))

    hand_on("L1 L7 L5 L3 R0 L2 R1 L6 R2 L4 R3")
    for i in (0,) + NEAR_FIRST:
        wait_for(left_ref, left_sem, along(i) * 2 + 1 - side)
    for i in range(8):
        pl.when(parity != i % 2)(
            lambda i=i: wait_for(right_ref, right_sem, i * 2 + core)
        )
        wait_for(right_ref, right_sem, i * 2 + 1 - core)
    staying = [move for move, _ in moves]
    for copy in sent:
        if not any(copy is move for move in staying):
            copy.wait_send()
    for move, stays in moves:
        pl.when(jnp.logical_not(stays))(move.wait_send)
    opposite(3).wait_send()


def stack_kernel(left_ref, right_ref, out_hbm, ready_ref, store_sem):
    def store(first):
        block = pl.ds(first, 2)
        return pltpu.make_async_copy(
            ready_ref.at[block], out_hbm.at[block], store_sem.at[first // 2]
        )

    def rows(ref, f, part):
        return jnp.concatenate(
            [ref[pl.ds(2 * f + part + h * 32, WINDOWS, stride=SLOT), :] for h in (0, 1)], axis=1
        )

    def stack(f):
        left = jnp.concatenate([rows(left_ref, f, 0), rows(left_ref, f, 1)], axis=0)
        left = (left * (1.0 / WINDOWS)).astype(jnp.bfloat16)
        real, imag = rows(right_ref, f, 0), rows(right_ref, f, 1)
        straight = jnp.concatenate([real, imag], axis=0).astype(jnp.bfloat16)
        turned = jnp.concatenate([-imag, real], axis=0).astype(jnp.bfloat16)
        for part, other in enumerate((straight, turned)):
            total = lax.dot_general(
                left, other, (((0,), (0,)), ((), ())), preferred_element_type=jnp.float32
            )
            ready_ref[f, part] = total.astype(ready_ref.dtype)

    for f in range(16):
        stack(f)
        if f % 2 == 2 - 1:
            store(f + 1 - 2).start()
    for first in range(0, 16, 2):
        store(first).wait()


def per_device(records, offsets, live_flags):
    channels, held = records.shape
    vmem = pl.BlockSpec(memory_space=pltpu.VMEM)
    hbm = pl.BlockSpec(memory_space=pltpu.HBM)
    gathered = jax.ShapeDtypeStruct((WINDOWS, SLOT, channels // 2), jnp.float32)
    left, right = pl.pallas_call(
        gather_kernel,
        out_shape=(gathered, gathered),
        in_specs=[hbm] * 4,
        out_specs=(vmem, vmem),
        scratch_shapes=[
            pltpu.VMEM((channels, held), jnp.bfloat16),
            pltpu.VMEM((2 * NB, held), jnp.float32),
            pltpu.SMEM((1,), jnp.int32),
            pltpu.VMEM((1, channels), jnp.int32),
            pltpu.SemaphoreType.DMA((4,)),
            pltpu.SemaphoreType.DMA((31,)),
            pltpu.SemaphoreType.DMA((WINDOWS,)),
            pltpu.SemaphoreType.DMA((WINDOWS,)),
            pltpu.SemaphoreType.DMA,
        ],
        compiler_params=pltpu.CompilerParams(
            collective_id=0, has_side_effects=True, vmem_limit_bytes=12 * 2**20
        ),
        name="gather_spectra",
    )(
        pltpu.with_memory_space_constraint(records, pltpu.HBM),
        pltpu.with_memory_space_constraint(dft_rows(held), pltpu.HBM),
        offsets,
        pltpu.with_memory_space_constraint(live_flags.reshape(1, channels), pltpu.HBM),
    )
    left = left.reshape(WINDOWS * SLOT, channels // 2)
    right = right.reshape(WINDOWS * SLOT, channels // 2)
    shape = (16, 2, channels, channels)
    return pl.pallas_call(
        stack_kernel,
        out_shape=jax.ShapeDtypeStruct(shape, jnp.bfloat16),
        in_specs=[vmem, vmem],
        out_specs=pl.BlockSpec(memory_space=pltpu.HBM),
        scratch_shapes=[
            pltpu.VMEM(shape, jnp.bfloat16),
            pltpu.SemaphoreType.DMA((8,)),
        ],
        compiler_params=pltpu.CompilerParams(vmem_limit_bytes=16 * 2**20),
        name="stack_windows",
    )(left, right)


def solution(mesh):
    in_specs = (P("row", "col"), P("col"), P("row"))
    out_specs = P("bin", None, "row", "col")
    return jax.shard_map(
        per_device, mesh=mesh, in_specs=in_specs, out_specs=out_specs, check_vma=False
    )
```
